32 devices in a mesh: groups: 2 (over x), hits: 8 (over z, y), heads: 2 (over core).
Axes of the slice: x: 2, y: 2, z: 4, core: 2. Of those that a mesh axis runs over, the one named last changes fastest.
Arguments:
- queries: bfloat16 [2048, 2048], P('groups', 'heads'), parts along dimension 0, may hold values from -13.5 to 13.5
- keys: bfloat16 [8192, 2048], P(('groups', 'hits'), 'heads'), parts along dimension 0, may hold values from -36 to 36
- values: bfloat16 [8192, 2048], P(('groups', 'hits'), 'heads'), parts along dimension 0, may hold values from -6 to 6
- hit_counts: int32 [16], P(('groups', 'hits')), parts along dimension 0, may hold values from 128 to 512, as said below
- latents: bfloat16 [2048, 2048], P(('groups', 'hits'), 'heads'), parts along dimension 0, may hold values from -23 to 23
- out_proj: bfloat16 [2048, 2048], P('heads'), may hold values from -1 to 1
- norm_gain: float32 [2048], P('heads'), may hold values from 0.1 to 1.9
- up_proj: bfloat16 [2048, 8192], P('heads', 'hits'), may hold values from -0.125 to 0.125
- down_proj: bfloat16 [8192, 2048], P('hits', 'heads'), may hold values from -0.25 to 0.25
Outputs:
- mixed: bfloat16 [2048, 2048], P(('groups', 'hits'), 'heads'), parts along dimension 0
The draws below stay inside these ranges and needn't reach their ends.
There are 2 independent parts, one for each index of `groups`. The reference program is written for one: setup_inputs(seed, part) draws one part's arguments, and reference() takes and returns one part's arrays. A program takes and returns all parts, laid end to end along the dimension named above; an argument that names none is the same for every part. Nothing has to cross between parts.
Inputs may be any that keep to these rules, and one draw needn't show every extreme that they name: hit_counts[s] live hits fill the first slots of shard s; some shard is full and some holds exactly 128.
All inputs are finite; a program needn't handle non-finite values.
Results may differ from the reference program's by a relative error of at most 0.012.
Values may be sent and summed in bfloat16 or wider, within the bound.
A program may use at most 64 MiB of HBM per device.

```python
import math
import jax
import jax.numpy as jnp
from jax import lax

L = 1024
D = 2048
NH = 16
HD = 128
F = 8192
HIT_DEV = 512
HITS = 4096
SHARDS = 8


def shared_draw(key):
    queries = 2.0 * jnp.clip(jax.random.normal(jax.random.fold_in(key, 11), (L, NH * HD), jnp.float32), -4.5, 4.5)
    keys = jnp.clip(jax.random.normal(jax.random.fold_in(key, 12), (HITS, NH * HD), jnp.float32), -4.5, 4.5)
    return (queries, keys)


def draw_queries(key, part):
    return shared_draw(key)[0].astype(jnp.bfloat16)


def draw_keys(key, part):
    return shared_draw(key)[1].astype(jnp.bfloat16)


def draw_hit_counts(key, part):
    counts = jax.random.randint(jax.random.fold_in(key, 21), (SHARDS,), HIT_DEV // 4, HIT_DEV + 1)
    order = jax.random.permutation(jax.random.fold_in(key, 22), SHARDS)
    counts = counts.at[order[0]].set(HIT_DEV)
    counts = counts.at[order[1]].set(HIT_DEV // 4)
    return counts.astype(jnp.int32)


def draw_latents(key, part):
    ramp = 0.2 * 10.0 ** (jnp.arange(D, dtype=jnp.float32) / (D - 1))
    jitter = jnp.exp(jax.random.uniform(jax.random.fold_in(key, 31), (D,), jnp.float32, jnp.log(0.7), jnp.log(1.4)))
    entries = jnp.clip(jax.random.normal(jax.random.fold_in(key, 32), (L, D), jnp.float32), -4.0, 4.0)
    row_scale = jnp.exp(jax.random.uniform(jax.random.fold_in(key, 33), (L,), jnp.float32, jnp.log(0.5), jnp.log(2.0)))
    return (entries * row_scale[:, None] * (ramp * jitter)[None, :]).astype(jnp.bfloat16)


def shard_levels(own_key, dims, pieces, smallest, top_value):
    def one(axis_at, shards_of):
        steps = jax.random.uniform(jax.random.fold_in(jax.random.fold_in(own_key, 6), axis_at), (shards_of,), jnp.float32, smallest / len(pieces), top_value / len(pieces))
        return jnp.repeat(jnp.exp(steps), dims[axis_at] // shards_of).reshape((-1,) + (1,) * (len(dims) - axis_at - 1))

    loudness = one(*pieces[0])
    for cut in pieces[1:]:
        loudness = loudness * one(*cut)
    return loudness


def centred(key, dims, width, bound, split=(), held_as=jnp.bfloat16):
    drawn = jax.random.normal(key, dims, jnp.float32) * width
    if len(split) > 0:
        drawn = shard_levels(key, dims, split, -0.22, 0.18) * drawn
    return jnp.clip(drawn, min=-bound, max=bound).astype(held_as)


def setup_inputs(seed: int = 0, part: int = 0) -> dict:
    key_of = jax.random.split(jax.random.key(seed), 10)
    own_keys = jax.random.split(jax.random.fold_in(key_of[9], part), 10)
    queries = draw_queries(jax.random.fold_in(jax.random.fold_in(key_of[9], part), 71), part)
    keys = draw_keys(jax.random.fold_in(jax.random.fold_in(key_of[9], part), 71), part)
    values = centred(own_keys[2], (HITS, NH * HD), 1.0, 6.0, ((0, 8), (1, 2)))
    hit_counts = draw_hit_counts(jax.random.fold_in(jax.random.fold_in(key_of[9], part), 71), part)
    latents = draw_latents(jax.random.fold_in(jax.random.fold_in(key_of[9], part), 71), part)
    out_proj = centred(key_of[5], (NH * HD, D), (max(D // 64, 8)) ** -0.5, 1.0, ((0, 2),))
    norm_gain = jnp.clip(1.0 + 0.18 * jax.random.normal(key_of[6], (D,), jnp.float32), 0.1, 1.9)
    up_proj = centred(key_of[7], (D, F), D ** -0.5, 0.125, ((0, 2), (1, 8)))
    down_proj = centred(key_of[8], (F, D), (max(F // 16, 8)) ** -0.5, 0.25, ((0, 8), (1, 2)))
    return dict(queries=queries, keys=keys, values=values, hit_counts=hit_counts, latents=latents, out_proj=out_proj, norm_gain=norm_gain, up_proj=up_proj, down_proj=down_proj)


def reference(queries, keys, values, hit_counts, latents, out_proj, norm_gain, up_proj, down_proj):
    positions = jnp.arange(HITS, dtype=jnp.int32)
    valid_hits = positions % HIT_DEV < hit_counts[positions // HIT_DEV]
    score_scale = 1.0 / math.sqrt(HD)

    def one_head(head_index):
        col_start = (head_index * HD).astype(jnp.int32)
        q_head = lax.dynamic_slice_in_dim(queries, col_start, HD, 1)
        k_head = lax.dynamic_slice_in_dim(keys, col_start, HD, 1)
        v_head = lax.dynamic_slice_in_dim(values, col_start, HD, 1)
        scores = lax.dot_general(q_head, k_head, (((1,), (1,)), ((), ())), preferred_element_type=jnp.float32) * score_scale
        scores = jnp.where(valid_hits[None, :], scores, -1e+30)
        row_top = lax.optimization_barrier(jnp.max(scores, axis=1))
        weights = jnp.where(valid_hits[None, :], jnp.exp(scores - row_top[:, None]), 0.0)
        row_total = lax.optimization_barrier(jnp.sum(weights, axis=1))
        context = jnp.dot(weights.astype(jnp.bfloat16), v_head, preferred_element_type=jnp.float32) / row_total[:, None]
        return context.astype(jnp.bfloat16)
    heads_out = lax.map(one_head, jnp.arange(NH, dtype=jnp.int32))
    context = heads_out.transpose(1, 0, 2).reshape(L, NH * HD)
    stream = latents.astype(jnp.float32) + jnp.dot(context, out_proj, preferred_element_type=jnp.float32)
    mean_square = lax.optimization_barrier(jnp.mean(stream * stream, axis=1))
    normed = (stream * lax.rsqrt(mean_square + 1e-06)[:, None] * norm_gain[None, :]).astype(jnp.bfloat16)
    hidden = jax.nn.gelu(jnp.dot(normed, up_proj, preferred_element_type=jnp.float32)).astype(jnp.bfloat16)
    mixed = stream + jnp.dot(hidden, down_proj, preferred_element_type=jnp.float32)
    return mixed.astype(jnp.bfloat16)
```

```python
import functools
import math

import jax
import jax.numpy as jnp
from jax import lax
from jax.experimental import pallas as pl
from jax.experimental.pallas import tpu as pltpu
from jax.sharding import PartitionSpec as P

HD = 128
LANES = 128
MESH = pl.DeviceIdType.MESH
F32 = jnp.float32
BF16 = jnp.bfloat16


def kernel(
    n,
    bias_ref, q_ref, k_ref, v_ref, lat_ref, gain_ref, wo_hbm, wu_hbm, wd_hbm,
    out_ref,
    wo, wu, wd,
    att_out, att_own, att_in, att_z, acc,
    psend, precv, sqs, sqr, stream,
    x_in, pu_own, pu_in, dy_out, dy_in, down_own, dz_in,
    w_sem, ay_s, ay_r, az_s, az_r, p_s, p_r, xz_s, xz_r, xy_s, xy_r, u_s, u_r, dy_s, dy_r, dz_s, dz_r,
):
    me = lax.axis_index("hits")
    core = lax.axis_index("heads")
    z, y = me // 2, me % 2
    outer = n // 2
    partner = z * 2 + (1 - y)
    sibling = 1 - core
    rows, width = q_ref.shape
    blk = rows // n
    heads = width // HD
    scale = math.log2(math.e) / math.sqrt(HD)
    features = wo.shape[1]

    def peer(zz):
        return lax.rem(zz + 2 * outer, outer) * 2 + y

    barrier = pltpu.get_barrier_semaphore()
    pl.semaphore_signal(barrier, inc=1, device_id={"hits": partner}, device_id_type=MESH)
    pl.semaphore_signal(barrier, inc=1, device_id={"heads": sibling}, device_id_type=MESH)
    for k in range(1, outer):
        pl.semaphore_signal(barrier, inc=1, device_id={"hits": peer(z + k)}, device_id_type=MESH)

    weights = [
        pltpu.make_async_copy(src, dst, w_sem.at[i])
        for i, (src, dst) in enumerate(((wo_hbm, wo), (wu_hbm, wu), (wd_hbm, wd)))
    ]
    for w in weights:
        w.start()

    def to_hits(src, dst, s, r, where):
        return pltpu.make_async_remote_copy(
            src_ref=src, dst_ref=dst, send_sem=s, recv_sem=r,
            device_id={"hits": where}, device_id_type=MESH,
        )

    def to_sibling(src, dst, s, r):
        return pltpu.make_async_remote_copy(
            src_ref=src, dst_ref=dst, send_sem=s, recv_sem=r,
            device_id={"heads": sibling}, device_id_type=MESH,
        )

    group = max(outer // 2, 1)
    tall = group * blk
    lane = lax.broadcasted_iota(jnp.int32, (tall, LANES), 1)

    def attend(chunk, half, dest):
        starts = []
        for g in range(group):
            zz = lax.rem(z + 1 + chunk * group + g, outer)
            starts.append(pl.multiple_of((zz * 2 + half) * blk, blk))
        stats = jnp.zeros((tall, LANES), F32)
        for h in range(heads):
            cols = slice(h * HD, (h + 1) * HD)
            q = jnp.concatenate([q_ref[pl.ds(s, blk), cols] for s in starts], axis=0)
            s = lax.dot_general(
                q, k_ref[:, cols], (((1,), (1,)), ((), ())), preferred_element_type=F32
            )
            s = s + bias_ref[...]
            top = (jnp.max(s, axis=1, keepdims=True) * scale).astype(BF16).astype(F32)
            p = jnp.exp2(s * scale - top)
            total = jnp.sum(p, axis=1, keepdims=True)
            o = jnp.dot(p.astype(BF16), v_ref[:, cols], preferred_element_type=F32).astype(BF16)
            high = total.astype(BF16).astype(F32)
            stats = jnp.where(lane == h, top, stats)
            stats = jnp.where(lane == heads + h, high, stats)
            stats = jnp.where(lane == 2 * heads + h, total - high, stats)
            for g in range(group):
                dest[chunk * group + g, :, cols] = o[g * blk:(g + 1) * blk]
        st = stats.astype(BF16)
        for g in range(group):
            dest[chunk * group + g, :, width:] = st[g * blk:(g + 1) * blk]

    def att_y(j):
        return to_hits(att_out.at[j], att_in.at[j], ay_s.at[j], ay_r.at[j], partner)

    def att_zc(j):
        return to_hits(att_own.at[j], att_z.at[j], az_s.at[j], az_r.at[j], peer(z + 1 + j))

    @pl.loop(0, outer // group)
    def _(chunk):
        attend(chunk, 1 - y, att_out)

        @pl.when(chunk == 0)
        def _():
            pl.semaphore_wait(barrier, outer + 1)

        for g in range(group):
            att_y(chunk * group + g).start()

    @pl.loop(0, outer // group)
    def _(chunk):
        attend(chunk, y, att_own)

    small = lax.broadcasted_iota(jnp.int32, (blk, LANES), 1)

    def columns(stats, h):
        top = stats[:, h:h + 1]
        total = stats[:, heads + h:heads + h + 1] + stats[:, 2 * heads + h:2 * heads + h + 1]
        return top, total

    @pl.loop(0, outer)
    def _(j):
        att_y(j).wait_recv()
        a = att_own[j, :, width:].astype(F32)
        b = att_in[j, :, width:].astype(F32)
        stats = jnp.zeros((blk, LANES), F32)
        for h in range(heads):
            cols = slice(h * HD, (h + 1) * HD)
            ta, la = columns(a, h)
            tb, lb = columns(b, h)
            top = jnp.maximum(ta, tb)
            fa, fb = jnp.exp2(ta - top), jnp.exp2(tb - top)
            total = la * fa + lb * fb
            high = total.astype(BF16).astype(F32)
            stats = jnp.where(small == h, top, stats)
            stats = jnp.where(small == heads + h, high, stats)
            stats = jnp.where(small == 2 * heads + h, total - high, stats)
            o = att_own[j, :, cols].astype(F32) * fa + att_in[j, :, cols].astype(F32) * fb
            att_own[j, :, cols] = o.astype(BF16)
        att_own[j, :, width:] = stats.astype(BF16)

        @pl.when(j < outer - 1)
        def _():
            att_zc(j).start()

    @pl.loop(0, outer - 1)
    def _(j):
        att_zc(j).wait_recv()

    parts = [(att_own, outer - 1)] + [(att_z, j) for j in range(outer - 1)]
    stat = [ref[j, :, width:].astype(F32) for ref, j in parts]
    for h in range(heads):
        cols = slice(h * HD, (h + 1) * HD)
        pairs = [columns(s, h) for s in stat]
        top = functools.reduce(jnp.maximum, [t for t, _ in pairs])
        factors = [jnp.exp2(t - top) for t, _ in pairs]
        total = sum(l * f for (_, l), f in zip(pairs, factors))
        o = sum(ref[j, :, cols].astype(F32) * f for (ref, j), f in zip(parts, factors))
        acc[:, cols] = (o / total).astype(BF16)

    weights[0].wait()
    theirs = pl.ds(pl.multiple_of(sibling * width, width), width)
    ours = pl.ds(pl.multiple_of(core * width, width), width)
    psend[...] = jnp.dot(acc[...], wo[:, theirs], preferred_element_type=F32)
    proj = to_sibling(psend, precv, p_s.at[0], p_r.at[0])
    proj.start()
    stream[...] = lat_ref[...].astype(F32) + jnp.dot(acc[...], wo[:, ours], preferred_element_type=F32)
    proj.wait_recv()
    summed = stream[...] + precv[...]
    stream[...] = summed
    own_sq = jnp.sum(summed * summed, axis=1, keepdims=True)
    sqs[...] = jnp.broadcast_to(own_sq, sqs.shape)
    squares = to_sibling(sqs, sqr, p_s.at[1], p_r.at[1])
    squares.start()
    squares.wait_recv()
    factor = lax.rsqrt((sqs[:, :1] + sqr[:, :1]) / features + 1e-06)
    x_in[0, 0] = (stream[...] * factor * gain_ref[...]).astype(BF16)

    def x_y(k):
        return to_hits(x_in.at[k, 0], x_in.at[k, 1], xy_s.at[k], xy_r.at[k], partner)

    def x_z(k):
        return to_hits(x_in.at[0, 0], x_in.at[k, 0], xz_s.at[k], xz_r.at[k], peer(z + k))

    def units(k):
        return to_sibling(pu_own.at[k], pu_in.at[k], u_s.at[k], u_r.at[k])

    def down_y(k):
        return to_hits(dy_out.at[k], dy_in.at[k], dy_s.at[k], dy_r.at[k], partner)

    def down_z(k):
        return to_hits(down_own.at[k], dz_in.at[k], dz_s.at[k], dz_r.at[k], peer(z - k))

    x_y(0).start()

    @pl.loop(1, outer)
    def _(k):
        x_z(k).start()

    weights[1].wait()
    weights[2].wait()

    @pl.loop(0, outer + 2)
    def _(k):
        @pl.when(k < outer)
        def _():
            x_y(k).wait_recv()
            x = x_in[k].reshape(2 * blk, width)
            pu_own[k] = jnp.dot(x, wu[...], preferred_element_type=F32)
            units(k).start()

        @pl.when(k < outer - 1)
        def _():
            x_z(k + 1).wait_recv()
            x_y(k + 1).start()

        @pl.when((k >= 1) & (k <= outer))
        def _():
            units(k - 1).wait_recv()
            hidden = jax.nn.gelu(pu_own[k - 1] + pu_in[k - 1]).astype(BF16)
            d = jnp.dot(hidden, wd[...], preferred_element_type=F32).astype(BF16)
            dy_out[k - 1] = d[blk:]
            down_y(k - 1).start()
            down_own[k - 1] = d[:blk]

        @pl.when(k >= 2)
        def _():
            down_y(k - 2).wait_recv()
            both = down_own[k - 2].astype(F32) + dy_in[k - 2].astype(F32)

            @pl.when(k == 2)
            def _():
                stream[...] = stream[...] + both

            @pl.when(k > 2)
            def _():
                down_own[k - 2] = both.astype(BF16)
                down_z(k - 2).start()

    @pl.loop(1, outer)
    def _(k):
        down_z(k).wait_recv()
        stream[...] = stream[...] + dz_in[k].astype(F32)

    out_ref[...] = stream[...].astype(BF16)

    proj.wait_send()
    squares.wait_send()

    @pl.loop(0, outer)
    def _(k):
        att_y(k).wait_send()
        x_y(k).wait_send()
        units(k).wait_send()
        down_y(k).wait_send()

    @pl.loop(1, outer)
    def _(k):
        att_zc(k - 1).wait_send()
        x_z(k).wait_send()
        down_z(k).wait_send()


def shards(n, queries, keys, values, hit_counts, latents, out_proj, norm_gain, up_proj, down_proj):
    rows, width = queries.shape
    blk = rows // n
    outer = n // 2
    hidden = up_proj.shape[1]
    features = out_proj.shape[1]
    live = lax.broadcasted_iota(jnp.int32, (1, keys.shape[0]), 1) < hit_counts[0]
    bias = jnp.where(live, 0.0, -1e30).astype(F32)
    vmem = pl.BlockSpec(memory_space=pltpu.VMEM)
    hbm = pl.BlockSpec(memory_space=pl.ANY)
    wide = width + LANES
    dma = lambda m: pltpu.SemaphoreType.DMA((m,))
    return pl.pallas_call(
        functools.partial(kernel, n),
        out_shape=jax.ShapeDtypeStruct(latents.shape, BF16),
        in_specs=[vmem] * 6 + [hbm] * 3,
        out_specs=vmem,
        scratch_shapes=[
            pltpu.VMEM(out_proj.shape, BF16),
            pltpu.VMEM(up_proj.shape, BF16),
            pltpu.VMEM(down_proj.shape, BF16),
            pltpu.VMEM((outer, blk, wide), BF16),
            pltpu.VMEM((outer, blk, wide), BF16),
            pltpu.VMEM((outer, blk, wide), BF16),
            pltpu.VMEM((outer - 1, blk, wide), BF16),
            pltpu.VMEM((blk, width), BF16),
            pltpu.VMEM((blk, width), F32),
            pltpu.VMEM((blk, width), F32),
            pltpu.VMEM((blk, LANES), F32),
            pltpu.VMEM((blk, LANES), F32),
            pltpu.VMEM((blk, width), F32),
            pltpu.VMEM((outer, 2, blk, width), BF16),
            pltpu.VMEM((outer, 2 * blk, hidden), F32),
            pltpu.VMEM((outer, 2 * blk, hidden), F32),
            pltpu.VMEM((outer, blk, width), BF16),
            pltpu.VMEM((outer, blk, width), BF16),
            pltpu.VMEM((outer, blk, width), BF16),
            pltpu.VMEM((outer, blk, width), BF16),
            dma(3),
            dma(outer), dma(outer), dma(outer), dma(outer),
            dma(2), dma(2),
            dma(outer), dma(outer), dma(outer), dma(outer),
            dma(outer), dma(outer), dma(outer), dma(outer), dma(outer), dma(outer),
        ],
        compiler_params=pltpu.CompilerParams(
            collective_id=0, has_side_effects=True, vmem_limit_bytes=56 * 1024 * 1024
        ),
        cost_estimate=pl.CostEstimate(
            flops=4 * rows * keys.shape[0] * width + 2 * blk * width * features + 4 * rows * width * hidden,
            bytes_accessed=16 * 1024 * 1024,
            transcendentals=rows * keys.shape[0] * (width // HD),
        ),
    )(bias, queries, keys, values, latents, norm_gain[None, :], out_proj, up_proj, down_proj)


def solution(mesh):
    return jax.shard_map(
        functools.partial(shards, mesh.shape["hits"]),
        mesh=mesh,
        in_specs=(
            P("groups", "heads"),
            P(("groups", "hits"), "heads"),
            P(("groups", "hits"), "heads"),
            P(("groups", "hits")),
            P(("groups", "hits"), "heads"),
            P("heads", None),
            P("heads"),
            P("heads", "hits"),
            P("hits", "heads"),
        ),
        out_specs=P(("groups", "hits"), "heads"),
        check_vma=False,
    )
```

```python
import functools
import math

import jax
import jax.numpy as jnp
from jax import lax
from jax.experimental import pallas as pl
from jax.experimental.pallas import tpu as pltpu
from jax.sharding import PartitionSpec as P

HD = 128
LANES = 128
MESH = pl.DeviceIdType.MESH
F32 = jnp.float32
BF16 = jnp.bfloat16


def kernel(
    n,
    bias_ref, q_ref, k_ref, v_ref, lat_ref, gain_ref, wo_hbm, wu_hbm, wd_hbm,
    out_ref,
    wo, wu, wd,
    att_out, att_own, att_in, att_z, acc,
    psend, precv, sqs, sqr, stream,
    x_in, pu_own, pu_in, dy_out, dy_in, down_own, dz_in,
    w_sem, ay_s, ay_r, az_s, az_r, p_s, p_r, xz_s, xz_r, xy_s, xy_r, u_s, u_r, dy_s, dy_r, dz_s, dz_r,
):
    me = lax.axis_index("hits")
    core = lax.axis_index("heads")
    z, y = me // 2, me % 2
    outer = n // 2
    partner = z * 2 + (1 - y)
    sibling = 1 - core
    rows, width = q_ref.shape
    blk = rows // n
    heads = width // HD
    scale = math.log2(math.e) / math.sqrt(HD)
    features = wo.shape[1]

    def peer(zz):
        return lax.rem(zz + 2 * outer, outer) * 2 + y

    barrier = pltpu.get_barrier_semaphore()
    pl.semaphore_signal(barrier, inc=1, device_id={"hits": partner}, device_id_type=MESH)
    pl.semaphore_signal(barrier, inc=1, device_id={"heads": sibling}, device_id_type=MESH)
    for k in range(1, outer):
        pl.semaphore_signal(barrier, inc=1, device_id={"hits": peer(z + k)}, device_id_type=MESH)

    weights = [
        pltpu.make_async_copy(src, dst, w_sem.at[i])
        for i, (src, dst) in enumerate(((wo_hbm, wo), (wu_hbm, wu), (wd_hbm, wd)))
    ]
    for w in weights:
        w.start()

    def to_hits(src, dst, s, r, where):
        return pltpu.make_async_remote_copy(
            src_ref=src, dst_ref=dst, send_sem=s, recv_sem=r,
            device_id={"hits": where}, device_id_type=MESH,
        )

    def to_sibling(src, dst, s, r):
        return pltpu.make_async_remote_copy(
            src_ref=src, dst_ref=dst, send_sem=s, recv_sem=r,
            device_id={"heads": sibling}, device_id_type=MESH,
        )

    group = max(outer // 2, 1)
    tall = group * blk
    lane = lax.broadcasted_iota(jnp.int32, (tall, LANES), 1)

    def attend(chunk, half, dest):
        starts = []
        for g in range(group):
            zz = lax.rem(z + 1 + chunk * group + g, outer)
            starts.append(pl.multiple_of((zz * 2 + half) * blk, blk))
        stats = jnp.zeros((tall, LANES), F32)
        for h in range(heads):
            cols = slice(h * HD, (h + 1) * HD)
            q = jnp.concatenate([q_ref[pl.ds(s, blk), cols] for s in starts], axis=0)
            s = lax.dot_general(
                q, k_ref[:, cols], (((1,), (1,)), ((), ())), preferred_element_type=F32
            )
            s = s + bias_ref[...]
            top = (jnp.max(s, axis=1, keepdims=True) * scale).astype(BF16).astype(F32)
            p = jnp.exp2(s * scale - top)
            total = jnp.sum(p, axis=1, keepdims=True)
            o = jnp.dot(p.astype(BF16), v_ref[:, cols], preferred_element_type=F32).astype(BF16)
            high = total.astype(BF16).astype(F32)
            stats = jnp.where(lane == h, top, stats)
            stats = jnp.where(lane == heads + h, high, stats)
            stats = jnp.where(lane == 2 * heads + h, total - high, stats)
            for g in range(group):
                dest[chunk * group + g, :, cols] = o[g * blk:(g + 1) * blk]
        st = stats.astype(BF16)
        for g in range(group):
            dest[chunk * group + g, :, width:] = st[g * blk:(g + 1) * blk]

    def att_y(j):
        return to_hits(att_out.at[j], att_in.at[j], ay_s.at[j], ay_r.at[j], partner)

    def att_zc(j):
        return to_hits(att_own.at[j], att_z.at[j], az_s.at[j], az_r.at[j], peer(z + 1 + j))

    @pl.loop(0, outer // group)
    def _(chunk):
        attend(chunk, 1 - y, att_out)

        @pl.when(chunk == 0)
        def _():
            pl.semaphore_wait(barrier, outer + 1)

        for g in range(group):
            att_y(chunk * group + g).start()

    @pl.loop(0, outer // group)
    def _(chunk):
        attend(chunk, y, att_own)

    small = lax.broadcasted_iota(jnp.int32, (blk, LANES), 1)

    def columns(stats, h):
        top = stats[:, h:h + 1]
        total = stats[:, heads + h:heads + h + 1] + stats[:, 2 * heads + h:2 * heads + h + 1]
        return top, total

    @pl.loop(0, outer)
    def _(j):
        att_y(j).wait_recv()
        a = att_own[j, :, width:].astype(F32)
        b = att_in[j, :, width:].astype(F32)
        stats = jnp.zeros((blk, LANES), F32)
        for h in range(heads):
            cols = slice(h * HD, (h + 1) * HD)
            ta, la = columns(a, h)
            tb, lb = columns(b, h)
            top = jnp.maximum(ta, tb)
            fa, fb = jnp.exp2(ta - top), jnp.exp2(tb - top)
            total = la * fa + lb * fb
            high = total.astype(BF16).astype(F32)
            stats = jnp.where(small == h, top, stats)
            stats = jnp.where(small == heads + h, high, stats)
            stats = jnp.where(small == 2 * heads + h, total - high, stats)
            o = att_own[j, :, cols].astype(F32) * fa + att_in[j, :, cols].astype(F32) * fb
            att_own[j, :, cols] = o.astype(BF16)
        att_own[j, :, width:] = stats.astype(BF16)

        @pl.when(j < outer - 1)
        def _():
            att_zc(j).start()

    @pl.loop(0, outer - 1)
    def _(j):
        att_zc(j).wait_recv()

    parts = [(att_own, outer - 1)] + [(att_z, j) for j in range(outer - 1)]
    stat = [ref[j, :, width:].astype(F32) for ref, j in parts]
    for h in range(heads):
        cols = slice(h * HD, (h + 1) * HD)
        pairs = [columns(s, h) for s in stat]
        top = functools.reduce(jnp.maximum, [t for t, _ in pairs])
        factors = [jnp.exp2(t - top) for t, _ in pairs]
        total = sum(l * f for (_, l), f in zip(pairs, factors))
        o = sum(ref[j, :, cols].astype(F32) * f for (ref, j), f in zip(parts, factors))
        acc[:, cols] = (o / total).astype(BF16)

    weights[0].wait()
    theirs = pl.ds(pl.multiple_of(sibling * width, width), width)
    ours = pl.ds(pl.multiple_of(core * width, width), width)
    psend[...] = jnp.dot(acc[...], wo[:, theirs], preferred_element_type=F32)
    proj = to_sibling(psend, precv, p_s.at[0], p_r.at[0])
    proj.start()
    stream[...] = lat_ref[...].astype(F32) + jnp.dot(acc[...], wo[:, ours], preferred_element_type=F32)
    proj.wait_recv()
    summed = stream[...] + precv[...]
    stream[...] = summed
    own_sq = jnp.sum(summed * summed, axis=1, keepdims=True)
    sqs[...] = jnp.broadcast_to(own_sq, sqs.shape)
    squares = to_sibling(sqs, sqr, p_s.at[1], p_r.at[1])
    squares.start()
    squares.wait_recv()
    factor = lax.rsqrt((sqs[:, :1] + sqr[:, :1]) / features + 1e-06)
    x_in[z, 0] = (stream[...] * factor * gain_ref[...]).astype(BF16)

    last = outer - 1
    near = jnp.minimum(z, last - z)
    longer = jnp.where(2 * z < last, 1, -1)

    def source(t):
        paired = z + (2 * lax.rem(t, 2) - 1) * ((t + 1) // 2)
        return jnp.where(t <= 2 * near, paired, z + longer * (t - near))

    def x_y(zs):
        return to_hits(x_in.at[zs, 0], x_in.at[zs, 1], xy_s.at[zs], xy_r.at[zs], partner)

    def x_right(zs):
        where = jnp.minimum(z + 1, last) * 2 + y
        return to_hits(x_in.at[zs, 0], x_in.at[zs, 0], xz_s.at[0, zs], xz_r.at[zs], where)

    def x_left(zs):
        where = jnp.maximum(z - 1, 0) * 2 + y
        return to_hits(x_in.at[zs, 0], x_in.at[zs, 0], xz_s.at[1, zs], xz_r.at[zs], where)

    def units(t):
        return to_sibling(pu_own.at[t], pu_in.at[t], u_s.at[t], u_r.at[t])

    def down_y(zs):
        return to_hits(dy_out.at[zs], dy_in.at[zs], dy_s.at[zs], dy_r.at[zs], partner)

    def down_z(zs):
        return to_hits(down_own.at[zs], dz_in.at[z], dz_s.at[zs], dz_r.at[z], zs * 2 + y)

    x_y(z).start()

    @pl.when(z < last)
    def _():
        x_right(z).start()

    @pl.when(z > 0)
    def _():
        x_left(z).start()

    weights[1].wait()
    weights[2].wait()

    @pl.loop(0, outer + 2)
    def _(t):
        @pl.when(t < outer)
        def _():
            zs = source(t)
            x_y(zs).wait_recv()
            x = x_in[zs].reshape(2 * blk, width)
            pu_own[t] = jnp.dot(x, wu[...], preferred_element_type=F32)
            units(t).start()

        @pl.when(z - t - 1 >= 0)
        def _():
            zs = z - t - 1
            x_right(zs).wait_recv()

            @pl.when(z < last)
            def _():
                x_right(zs).start()

        @pl.when(z + t + 1 <= last)
        def _():
            zs = z + t + 1
            x_left(zs).wait_recv()

            @pl.when(z > 0)
            def _():
                x_left(zs).start()

        @pl.when(t < last)
        def _():
            x_y(source(t + 1)).start()

        @pl.when((t >= 1) & (t <= outer))
        def _():
            zs = source(t - 1)
            units(t - 1).wait_recv()
            hidden = jax.nn.gelu(pu_own[t - 1] + pu_in[t - 1]).astype(BF16)
            d = jnp.dot(hidden, wd[...], preferred_element_type=F32).astype(BF16)
            dy_out[zs] = d[blk:]
            down_own[zs] = d[:blk]

            @pl.when(t > 1)
            def _():
                down_y(zs).start()

            @pl.when(t == outer)
            def _():
                down_y(z).start()

        @pl.when(t > 2)
        def _():
            zs = source(t - 2)
            down_y(zs).wait_recv()
            both = down_own[zs].astype(F32) + dy_in[zs].astype(F32)
            down_own[zs] = both.astype(BF16)
            down_z(zs).start()

    down_y(z).wait_recv()
    stream[...] = stream[...] + down_own[z].astype(F32) + dy_in[z].astype(F32)

    @pl.loop(1, outer)
    def _(t):
        zs = source(t)
        to_hits(down_own.at[zs], dz_in.at[zs], dz_s.at[zs], dz_r.at[zs], zs * 2 + y).wait_recv()
        stream[...] = stream[...] + dz_in[zs].astype(F32)

    out_ref[...] = stream[...].astype(BF16)

    proj.wait_send()
    squares.wait_send()

    @pl.loop(0, outer)
    def _(t):
        att_y(t).wait_send()
        x_y(t).wait_send()
        units(t).wait_send()
        down_y(t).wait_send()

        @pl.when(t != z)
        def _():
            down_z(t).wait_send()

        @pl.when((t <= z) & (z < last))
        def _():
            x_right(t).wait_send()

        @pl.when((t >= z) & (z > 0))
        def _():
            x_left(t).wait_send()

    @pl.loop(0, last)
    def _(j):
        att_zc(j).wait_send()


def shards(n, queries, keys, values, hit_counts, latents, out_proj, norm_gain, up_proj, down_proj):
    rows, width = queries.shape
    blk = rows // n
    outer = n // 2
    hidden = up_proj.shape[1]
    features = out_proj.shape[1]
    live = lax.broadcasted_iota(jnp.int32, (1, keys.shape[0]), 1) < hit_counts[0]
    bias = jnp.where(live, 0.0, -1e30).astype(F32)
    vmem = pl.BlockSpec(memory_space=pltpu.VMEM)
    hbm = pl.BlockSpec(memory_space=pl.ANY)
    wide = width + LANES
    dma = lambda m: pltpu.SemaphoreType.DMA((m,))
    return pl.pallas_call(
        functools.partial(kernel, n),
        out_shape=jax.ShapeDtypeStruct(latents.shape, BF16),
        in_specs=[vmem] * 6 + [hbm] * 3,
        out_specs=vmem,
        scratch_shapes=[
            pltpu.VMEM(out_proj.shape, BF16),
            pltpu.VMEM(up_proj.shape, BF16),
            pltpu.VMEM(down_proj.shape, BF16),
            pltpu.VMEM((outer, blk, wide), BF16),
            pltpu.VMEM((outer, blk, wide), BF16),
            pltpu.VMEM((outer, blk, wide), BF16),
            pltpu.VMEM((outer - 1, blk, wide), BF16),
            pltpu.VMEM((blk, width), BF16),
            pltpu.VMEM((blk, width), F32),
            pltpu.VMEM((blk, width), F32),
            pltpu.VMEM((blk, LANES), F32),
            pltpu.VMEM((blk, LANES), F32),
            pltpu.VMEM((blk, width), F32),
            pltpu.VMEM((outer, 2, blk, width), BF16),
            pltpu.VMEM((outer, 2 * blk, hidden), F32),
            pltpu.VMEM((outer, 2 * blk, hidden), F32),
            pltpu.VMEM((outer, blk, width), BF16),
            pltpu.VMEM((outer, blk, width), BF16),
            pltpu.VMEM((outer, blk, width), BF16),
            pltpu.VMEM((outer, blk, width), BF16),
            dma(3),
            dma(outer), dma(outer), dma(outer), dma(outer),
            dma(2), dma(2),
            pltpu.SemaphoreType.DMA((2, outer)), dma(outer), dma(outer), dma(outer),
            dma(outer), dma(outer), dma(outer), dma(outer), dma(outer), dma(outer),
        ],
        compiler_params=pltpu.CompilerParams(
            collective_id=0, has_side_effects=True, vmem_limit_bytes=56 * 1024 * 1024
        ),
        cost_estimate=pl.CostEstimate(
            flops=4 * rows * keys.shape[0] * width + 2 * blk * width * features + 4 * rows * width * hidden,
            bytes_accessed=16 * 1024 * 1024,
            transcendentals=rows * keys.shape[0] * (width // HD),
        ),
    )(bias, queries, keys, values, latents, norm_gain[None, :], out_proj, up_proj, down_proj)


def solution(mesh):
    return jax.shard_map(
        functools.partial(shards, mesh.shape["hits"]),
        mesh=mesh,
        in_specs=(
            P("groups", "heads"),
            P(("groups", "hits"), "heads"),
            P(("groups", "hits"), "heads"),
            P(("groups", "hits")),
            P(("groups", "hits"), "heads"),
            P("heads", None),
            P("heads"),
            P("heads", "hits"),
            P("hits", "heads"),
        ),
        out_specs=P(("groups", "hits"), "heads"),
        check_vma=False,
    )
```

```python
import functools
import math

import jax
import jax.numpy as jnp
from jax import lax
from jax.experimental import pallas as pl
from jax.experimental.pallas import tpu as pltpu
from jax.sharding import PartitionSpec as P

HD = 128
LANES = 128
MESH = pl.DeviceIdType.MESH
F32 = jnp.float32
BF16 = jnp.bfloat16


def kernel(
    n,
    bias_ref, q_ref, k_ref, v_ref, lat_ref, gain_ref, wo_hbm, wu_hbm, wd_hbm,
    out_ref,
    wo, wu, wd,
    att_out, att_own, att_in, att_z, st_out, st_own, st_in, st_z, acc,
    psend, precv, sqs, sqr, stream,
    x_in, pu_own, pu_in, dy_out, dy_in, down_own, dz_in,
    w_sem, ay_s, ay_r, az_s, az_r, sy_s, sy_r, sz_s, sz_r, p_s, p_r, xz_s, xz_r, xy_s, xy_r, u_s, u_r, dy_s, dy_r, dz_s, dz_r,
):
    me = lax.axis_index("hits")
    core = lax.axis_index("heads")
    z, y = me // 2, me % 2
    outer = n // 2
    partner = z * 2 + (1 - y)
    sibling = 1 - core
    rows, width = q_ref.shape
    blk = rows // n
    heads = width // HD
    scale = math.log2(math.e) / math.sqrt(HD)
    features = wo.shape[1]

    def peer(zz):
        return lax.rem(zz + 2 * outer, outer) * 2 + y

    barrier = pltpu.get_barrier_semaphore()
    pl.semaphore_signal(barrier, inc=1, device_id={"hits": partner}, device_id_type=MESH)
    pl.semaphore_signal(barrier, inc=1, device_id={"heads": sibling}, device_id_type=MESH)
    for k in range(1, outer):
        pl.semaphore_signal(barrier, inc=1, device_id={"hits": peer(z + k)}, device_id_type=MESH)

    weights = [
        pltpu.make_async_copy(src, dst, w_sem.at[i])
        for i, (src, dst) in enumerate(((wo_hbm, wo), (wu_hbm, wu), (wd_hbm, wd)))
    ]
    for w in weights:
        w.start()

    def to_hits(src, dst, s, r, where):
        return pltpu.make_async_remote_copy(
            src_ref=src, dst_ref=dst, send_sem=s, recv_sem=r,
            device_id={"hits": where}, device_id_type=MESH,
        )

    def to_sibling(src, dst, s, r):
        return pltpu.make_async_remote_copy(
            src_ref=src, dst_ref=dst, send_sem=s, recv_sem=r,
            device_id={"heads": sibling}, device_id_type=MESH,
        )

    last = outer - 1
    near = jnp.minimum(z, last - z)
    longer = jnp.where(2 * z < last, 1, -1)

    def source(t):
        paired = z + (2 * lax.rem(t, 2) - 1) * ((t + 1) // 2)
        return jnp.where(t <= 2 * near, paired, z + longer * (t - near))

    group = max(outer // 2, 1)
    tall = group * blk
    lane = lax.broadcasted_iota(jnp.int32, (tall, LANES), 1)

    def attend(chunk, half, dest, stat_dest):
        owners = [source(last - (chunk * group + g)) for g in range(group)]
        starts = [pl.multiple_of((zz * 2 + half) * blk, blk) for zz in owners]
        stats = jnp.zeros((tall, LANES), F32)
        for h in range(heads):
            cols = slice(h * HD, (h + 1) * HD)
            q = jnp.concatenate([q_ref[pl.ds(s, blk), cols] for s in starts], axis=0)
            s = lax.dot_general(
                q, k_ref[:, cols], (((1,), (1,)), ((), ())), preferred_element_type=F32
            )
            s = s + bias_ref[...]
            top = jnp.max(s, axis=1, keepdims=True) * scale
            p = jnp.exp2(s * scale - top)
            total = jnp.sum(p, axis=1, keepdims=True)
            o = jnp.dot(p.astype(BF16), v_ref[:, cols], preferred_element_type=F32).astype(BF16)
            stats = jnp.where(lane == h, top, stats)
            stats = jnp.where(lane == heads + h, total, stats)
            for g in range(group):
                dest[owners[g], :, cols] = o[g * blk:(g + 1) * blk]
        for g in range(group):
            stat_dest[owners[g]] = stats[g * blk:(g + 1) * blk].T[:2 * heads]

    def att_y(d):
        return (
            to_hits(st_out.at[d], st_in.at[d], sy_s.at[d], sy_r.at[d], partner),
            to_hits(att_out.at[d], att_in.at[d], ay_s.at[d], ay_r.at[d], partner),
        )

    def att_z_step(side, d):
        zz = jnp.minimum(z + 1, last) if side == 0 else jnp.maximum(z - 1, 0)
        where = zz * 2 + y
        return (
            to_hits(st_own.at[d], st_z.at[side, d], sz_s.at[d], sz_r.at[side, d], where),
            to_hits(att_own.at[d], att_z.at[side, d], az_s.at[d], az_r.at[side, d], where),
        )

    @pl.loop(0, outer // group)
    def _(chunk):
        attend(chunk, 1 - y, att_out, st_out)

        @pl.when(chunk == 0)
        def _():
            pl.semaphore_wait(barrier, outer + 1)

        for g in range(group):
            for c in att_y(source(last - (chunk * group + g))):
                c.start()

    @pl.loop(0, outer // group)
    def _(chunk):
        attend(chunk, y, att_own, st_own)

    def spread(rows_of):
        pad = jnp.zeros((LANES - sum(r.shape[0] for r in rows_of), blk), F32)
        return jnp.concatenate(rows_of + [pad], axis=0).T

    def merge(d, values, stats):
        a, b = st_own[d], stats
        ta, la, tb, lb = a[:heads], a[heads:], b[:heads], b[heads:]
        top = jnp.maximum(ta, tb)
        fa, fb = jnp.exp2(ta - top), jnp.exp2(tb - top)
        st_own[d] = jnp.concatenate([top, la * fa + lb * fb], axis=0)
        f = spread([fa, fb])
        for h in range(heads):
            cols = slice(h * HD, (h + 1) * HD)
            o = att_own[d, :, cols].astype(F32) * f[:, h:h + 1]
            o = o + values[:, cols].astype(F32) * f[:, heads + h:heads + h + 1]
            att_own[d, :, cols] = o.astype(BF16)

    @pl.loop(0, outer)
    def _(j):
        d = source(last - j)
        for c in att_y(d):
            c.wait_recv()
        merge(d, att_in.at[d], st_in[d])

        for side, arrives in ((0, (d >= z) & (z > 0)), (1, (d <= z) & (z < last))):
            @pl.when(arrives)
            def _():
                for c in att_z_step(side, d):
                    c.wait_recv()
                merge(d, att_z.at[side, d], st_z[side, d])

        for side, leaves in ((0, d > z), (1, d < z)):
            @pl.when(leaves)
            def _():
                for c in att_z_step(side, d):
                    c.start()

    inverse = spread([1.0 / st_own[z][heads:]])
    for h in range(heads):
        cols = slice(h * HD, (h + 1) * HD)
        acc[:, cols] = (att_own[z, :, cols].astype(F32) * inverse[:, h:h + 1]).astype(BF16)

    weights[0].wait()
    theirs = pl.ds(pl.multiple_of(sibling * width, width), width)
    ours = pl.ds(pl.multiple_of(core * width, width), width)
    psend[...] = jnp.dot(acc[...], wo[:, theirs], preferred_element_type=F32)
    proj = to_sibling(psend, precv, p_s.at[0], p_r.at[0])
    proj.start()
    stream[...] = lat_ref[...].astype(F32) + jnp.dot(acc[...], wo[:, ours], preferred_element_type=F32)
    proj.wait_recv()
    summed = stream[...] + precv[...]
    stream[...] = summed
    own_sq = jnp.sum(summed * summed, axis=1, keepdims=True)
    sqs[...] = jnp.broadcast_to(own_sq, sqs.shape)
    squares = to_sibling(sqs, sqr, p_s.at[1], p_r.at[1])
    squares.start()
    squares.wait_recv()
    factor = lax.rsqrt((sqs[:, :1] + sqr[:, :1]) / features + 1e-06)
    x_in[z, 0] = (stream[...] * factor * gain_ref[...]).astype(BF16)

    def x_y(zs):
        return to_hits(x_in.at[zs, 0], x_in.at[zs, 1], xy_s.at[zs], xy_r.at[zs], partner)

    def x_right(zs):
        where = jnp.minimum(z + 1, last) * 2 + y
        return to_hits(x_in.at[zs, 0], x_in.at[zs, 0], xz_s.at[0, zs], xz_r.at[zs], where)

    def x_left(zs):
        where = jnp.maximum(z - 1, 0) * 2 + y
        return to_hits(x_in.at[zs, 0], x_in.at[zs, 0], xz_s.at[1, zs], xz_r.at[zs], where)

    def units(t):
        return to_sibling(pu_own.at[t], pu_in.at[t], u_s.at[t], u_r.at[t])

    def down_y(zs):
        return to_hits(dy_out.at[zs], dy_in.at[zs], dy_s.at[zs], dy_r.at[zs], partner)

    def down_z(zs):
        return to_hits(down_own.at[zs], dz_in.at[z], dz_s.at[zs], dz_r.at[z], zs * 2 + y)

    x_y(z).start()

    @pl.when(z < last)
    def _():
        x_right(z).start()

    @pl.when(z > 0)
    def _():
        x_left(z).start()

    weights[1].wait()
    weights[2].wait()

    @pl.loop(0, outer + 2)
    def _(t):
        @pl.when(t < outer)
        def _():
            zs = source(t)
            x_y(zs).wait_recv()
            x = x_in[zs].reshape(2 * blk, width)
            pu_own[t] = jnp.dot(x, wu[...], preferred_element_type=F32)
            units(t).start()

        @pl.when(z - t - 1 >= 0)
        def _():
            zs = z - t - 1
            x_right(zs).wait_recv()

            @pl.when(z < last)
            def _():
                x_right(zs).start()

        @pl.when(z + t + 1 <= last)
        def _():
            zs = z + t + 1
            x_left(zs).wait_recv()

            @pl.when(z > 0)
            def _():
                x_left(zs).start()

        @pl.when(t < last)
        def _():
            x_y(source(t + 1)).start()

        @pl.when((t >= 1) & (t <= outer))
        def _():
            zs = source(t - 1)
            units(t - 1).wait_recv()
            hidden = jax.nn.gelu(pu_own[t - 1] + pu_in[t - 1]).astype(BF16)
            d = jnp.dot(hidden, wd[...], preferred_element_type=F32).astype(BF16)
            dy_out[zs] = d[blk:]
            down_own[zs] = d[:blk]

            @pl.when(t > 1)
            def _():
                down_y(zs).start()

            @pl.when(t == outer)
            def _():
                down_y(z).start()

        @pl.when(t > 2)
        def _():
            zs = source(t - 2)
            down_y(zs).wait_recv()
            both = down_own[zs].astype(F32) + dy_in[zs].astype(F32)
            down_own[zs] = both.astype(BF16)
            down_z(zs).start()

    down_y(z).wait_recv()
    stream[...] = stream[...] + down_own[z].astype(F32) + dy_in[z].astype(F32)

    @pl.loop(1, outer)
    def _(t):
        zs = source(t)
        to_hits(down_own.at[zs], dz_in.at[zs], dz_s.at[zs], dz_r.at[zs], zs * 2 + y).wait_recv()
        stream[...] = stream[...] + dz_in[zs].astype(F32)

    out_ref[...] = stream[...].astype(BF16)

    proj.wait_send()
    squares.wait_send()

    @pl.loop(0, outer)
    def _(t):
        for c in att_y(t):
            c.wait_send()

        x_y(t).wait_send()
        units(t).wait_send()
        down_y(t).wait_send()

        @pl.when(t != z)
        def _():
            down_z(t).wait_send()
            for c in att_z_step(0, t):
                c.wait_send()

        @pl.when((t <= z) & (z < last))
        def _():
            x_right(t).wait_send()

        @pl.when((t >= z) & (z > 0))
        def _():
            x_left(t).wait_send()


def shards(n, queries, keys, values, hit_counts, latents, out_proj, norm_gain, up_proj, down_proj):
    rows, width = queries.shape
    blk = rows // n
    outer = n // 2
    hidden = up_proj.shape[1]
    features = out_proj.shape[1]
    live = lax.broadcasted_iota(jnp.int32, (1, keys.shape[0]), 1) < hit_counts[0]
    bias = jnp.where(live, 0.0, -1e30).astype(F32)
    vmem = pl.BlockSpec(memory_space=pltpu.VMEM)
    hbm = pl.BlockSpec(memory_space=pl.ANY)
    heads = width // HD
    dma = lambda m: pltpu.SemaphoreType.DMA((m,))
    return pl.pallas_call(
        functools.partial(kernel, n),
        out_shape=jax.ShapeDtypeStruct(latents.shape, BF16),
        in_specs=[vmem] * 6 + [hbm] * 3,
        out_specs=vmem,
        scratch_shapes=[
            pltpu.VMEM(out_proj.shape, BF16),
            pltpu.VMEM(up_proj.shape, BF16),
            pltpu.VMEM(down_proj.shape, BF16),
            pltpu.VMEM((outer, blk, width), BF16),
            pltpu.VMEM((outer, blk, width), BF16),
            pltpu.VMEM((outer, blk, width), BF16),
            pltpu.VMEM((2, outer, blk, width), BF16),
            pltpu.VMEM((outer, 2 * heads, blk), F32),
            pltpu.VMEM((outer, 2 * heads, blk), F32),
            pltpu.VMEM((outer, 2 * heads, blk), F32),
            pltpu.VMEM((2, outer, 2 * heads, blk), F32),
            pltpu.VMEM((blk, width), BF16),
            pltpu.VMEM((blk, width), F32),
            pltpu.VMEM((blk, width), F32),
            pltpu.VMEM((blk, LANES), F32),
            pltpu.VMEM((blk, LANES), F32),
            pltpu.VMEM((blk, width), F32),
            pltpu.VMEM((outer, 2, blk, width), BF16),
            pltpu.VMEM((outer, 2 * blk, hidden), F32),
            pltpu.VMEM((outer, 2 * blk, hidden), F32),
            pltpu.VMEM((outer, blk, width), BF16),
            pltpu.VMEM((outer, blk, width), BF16),
            pltpu.VMEM((outer, blk, width), BF16),
            pltpu.VMEM((outer, blk, width), BF16),
            dma(3),
            dma(outer), dma(outer), dma(outer), pltpu.SemaphoreType.DMA((2, outer)),
            dma(outer), dma(outer), dma(outer), pltpu.SemaphoreType.DMA((2, outer)),
            dma(2), dma(2),
            pltpu.SemaphoreType.DMA((2, outer)), dma(outer), dma(outer), dma(outer),
            dma(outer), dma(outer), dma(outer), dma(outer), dma(outer), dma(outer),
        ],
        compiler_params=pltpu.CompilerParams(
            collective_id=0, has_side_effects=True, vmem_limit_bytes=56 * 1024 * 1024
        ),
        cost_estimate=pl.CostEstimate(
            flops=4 * rows * keys.shape[0] * width + 2 * blk * width * features + 4 * rows * width * hidden,
            bytes_accessed=16 * 1024 * 1024,
            transcendentals=rows * keys.shape[0] * (width // HD),
        ),
    )(bias, queries, keys, values, latents, norm_gain[None, :], out_proj, up_proj, down_proj)


def solution(mesh):
    return jax.shard_map(
        functools.partial(shards, mesh.shape["hits"]),
        mesh=mesh,
        in_specs=(
            P("groups", "heads"),
            P(("groups", "hits"), "heads"),
            P(("groups", "hits"), "heads"),
            P(("groups", "hits")),
            P(("groups", "hits"), "heads"),
            P("heads", None),
            P("heads"),
            P("heads", "hits"),
            P("hits", "heads"),
        ),
        out_specs=P(("groups", "hits"), "heads"),
        check_vma=False,
    )
```

```python
import functools
import math

import jax
import jax.numpy as jnp
from jax import lax
from jax.experimental import pallas as pl
from jax.experimental.pallas import tpu as pltpu
from jax.sharding import PartitionSpec as P

HD = 128
LANES = 128
MESH = pl.DeviceIdType.MESH
F32 = jnp.float32
BF16 = jnp.bfloat16


def kernel(
    n,
    bias_ref, q_ref, k_ref, v_ref, lat_ref, gain_ref, wo_hbm, wu_hbm, wd_hbm,
    out_ref,
    wo, wu, wd,
    att_out, att_own, att_in, att_z, st_out, st_own, st_in, st_z, acc,
    psend, precv, sqs, sqr, stream,
    x_in, pu_own, pu_in, dy_out, dy_in, down_own, dz_in,
    w_sem, ay_s, ay_r, az_s, az_r, sy_s, sy_r, sz_s, sz_r, p_s, p_r, xz_s, xz_r, xy_s, xy_r, u_s, u_r, dy_s, dy_r, dz_s, dz_r,
):
    me = lax.axis_index("hits")
    core = lax.axis_index("heads")
    z, y = me // 2, me % 2
    outer = n // 2
    partner = z * 2 + (1 - y)
    sibling = 1 - core
    rows, width = q_ref.shape
    blk = rows // n
    heads = width // HD
    scale = math.log2(math.e) / math.sqrt(HD)
    features = wo.shape[1]

    def peer(zz):
        return lax.rem(zz + 2 * outer, outer) * 2 + y

    barrier = pltpu.get_barrier_semaphore()
    pl.semaphore_signal(barrier, inc=1, device_id={"hits": partner}, device_id_type=MESH)
    pl.semaphore_signal(barrier, inc=1, device_id={"heads": sibling}, device_id_type=MESH)
    for k in range(1, outer):
        pl.semaphore_signal(barrier, inc=1, device_id={"hits": peer(z + k)}, device_id_type=MESH)

    weights = [
        pltpu.make_async_copy(src, dst, w_sem.at[i])
        for i, (src, dst) in enumerate(((wo_hbm, wo), (wu_hbm, wu), (wd_hbm, wd)))
    ]
    for w in weights:
        w.start()

    def to_hits(src, dst, s, r, where):
        return pltpu.make_async_remote_copy(
            src_ref=src, dst_ref=dst, send_sem=s, recv_sem=r,
            device_id={"hits": where}, device_id_type=MESH,
        )

    def to_sibling(src, dst, s, r):
        return pltpu.make_async_remote_copy(
            src_ref=src, dst_ref=dst, send_sem=s, recv_sem=r,
            device_id={"heads": sibling}, device_id_type=MESH,
        )

    last = outer - 1
    near = jnp.minimum(z, last - z)
    longer = jnp.where(2 * z < last, 1, -1)

    def source(t):
        paired = z + (2 * lax.rem(t, 2) - 1) * ((t + 1) // 2)
        return jnp.where(t <= 2 * near, paired, z + longer * (t - near))

    group = max(outer // 2, 1)
    tall = group * blk
    lane = lax.broadcasted_iota(jnp.int32, (tall, LANES), 1)

    def attend(chunk, half, dest, stat_dest):
        owners = [source(last - (chunk * group + g)) for g in range(group)]
        starts = [pl.multiple_of((zz * 2 + half) * blk, blk) for zz in owners]
        stats = jnp.zeros((tall, LANES), F32)
        for h in range(heads):
            cols = slice(h * HD, (h + 1) * HD)
            q = jnp.concatenate([q_ref[pl.ds(s, blk), cols] for s in starts], axis=0)
            s = lax.dot_general(
                q, k_ref[:, cols], (((1,), (1,)), ((), ())), preferred_element_type=F32
            )
            s = s + bias_ref[...]
            top = jnp.max(s, axis=1, keepdims=True) * scale
            p = jnp.exp2(s * scale - top)
            total = jnp.sum(p, axis=1, keepdims=True)
            o = jnp.dot(p.astype(BF16), v_ref[:, cols], preferred_element_type=F32).astype(BF16)
            stats = jnp.where(lane == h, top, stats)
            stats = jnp.where(lane == heads + h, total, stats)
            for g in range(group):
                dest[owners[g], :, cols] = o[g * blk:(g + 1) * blk]
        for g in range(group):
            stat_dest[owners[g]] = stats[g * blk:(g + 1) * blk].T[:2 * heads]

    def att_y(d):
        return (
            to_hits(st_out.at[d], st_in.at[d], sy_s.at[d], sy_r.at[d], partner),
            to_hits(att_out.at[d], att_in.at[d], ay_s.at[d], ay_r.at[d], partner),
        )

    def att_z_step(side, d):
        zz = jnp.minimum(z + 1, last) if side == 0 else jnp.maximum(z - 1, 0)
        where = zz * 2 + y
        return (
            to_hits(st_own.at[d], st_z.at[side, d], sz_s.at[d], sz_r.at[side, d], where),
            to_hits(att_own.at[d], att_z.at[side, d], az_s.at[d], az_r.at[side, d], where),
        )

    @pl.loop(0, outer // group)
    def _(chunk):
        attend(chunk, 1 - y, att_out, st_out)

        @pl.when(chunk == 0)
        def _():
            pl.semaphore_wait(barrier, outer + 1)

        for g in range(group):
            for c in att_y(source(last - (chunk * group + g))):
                c.start()

    @pl.loop(0, outer // group)
    def _(chunk):
        attend(chunk, y, att_own, st_own)

    def spread(rows_of):
        pad = jnp.zeros((LANES - sum(r.shape[0] for r in rows_of), blk), F32)
        return jnp.concatenate(rows_of + [pad], axis=0).T

    def merge(d, values, stats):
        a, b = st_own[d], stats
        ta, la, tb, lb = a[:heads], a[heads:], b[:heads], b[heads:]
        top = jnp.maximum(ta, tb)
        fa, fb = jnp.exp2(ta - top), jnp.exp2(tb - top)
        st_own[d] = jnp.concatenate([top, la * fa + lb * fb], axis=0)
        f = spread([fa, fb])
        for h in range(heads):
            cols = slice(h * HD, (h + 1) * HD)
            o = att_own[d, :, cols].astype(F32) * f[:, h:h + 1]
            o = o + values[:, cols].astype(F32) * f[:, heads + h:heads + h + 1]
            att_own[d, :, cols] = o.astype(BF16)

    @pl.loop(0, outer)
    def _(j):
        d = source(last - j)
        for c in att_y(d):
            c.wait_recv()
        merge(d, att_in.at[d], st_in[d])

        for side, arrives in ((0, (d >= z) & (z > 0)), (1, (d <= z) & (z < last))):
            @pl.when(arrives)
            def _():
                for c in att_z_step(side, d):
                    c.wait_recv()
                merge(d, att_z.at[side, d], st_z[side, d])

        for side, leaves in ((0, d > z), (1, d < z)):
            @pl.when(leaves)
            def _():
                for c in att_z_step(side, d):
                    c.start()

    inverse = spread([1.0 / st_own[z][heads:]])
    for h in range(heads):
        cols = slice(h * HD, (h + 1) * HD)
        acc[:, cols] = (att_own[z, :, cols].astype(F32) * inverse[:, h:h + 1]).astype(BF16)

    weights[0].wait()
    theirs = pl.ds(pl.multiple_of(sibling * width, width), width)
    ours = pl.ds(pl.multiple_of(core * width, width), width)
    psend[...] = jnp.dot(acc[...], wo[:, theirs], preferred_element_type=F32)
    proj = to_sibling(psend, precv, p_s.at[0], p_r.at[0])
    proj.start()
    stream[...] = lat_ref[...].astype(F32) + jnp.dot(acc[...], wo[:, ours], preferred_element_type=F32)
    proj.wait_recv()
    summed = stream[...] + precv[...]
    stream[...] = summed
    own_sq = jnp.sum(summed * summed, axis=1, keepdims=True)
    sqs[...] = jnp.broadcast_to(own_sq, sqs.shape)
    squares = to_sibling(sqs, sqr, p_s.at[1], p_r.at[1])
    squares.start()
    squares.wait_recv()
    factor = lax.rsqrt((sqs[:, :1] + sqr[:, :1]) / features + 1e-06)
    x_in[z, 0] = (stream[...] * factor * gain_ref[...]).astype(BF16)

    def x_y(zs):
        return to_hits(x_in.at[zs, 0], x_in.at[zs, 1], xy_s.at[zs], xy_r.at[zs], partner)

    def x_right(zs):
        where = jnp.minimum(z + 1, last) * 2 + y
        return to_hits(x_in.at[zs, 0], x_in.at[zs, 0], xz_s.at[0, zs], xz_r.at[zs], where)

    def x_left(zs):
        where = jnp.maximum(z - 1, 0) * 2 + y
        return to_hits(x_in.at[zs, 0], x_in.at[zs, 0], xz_s.at[1, zs], xz_r.at[zs], where)

    def units(t):
        return to_sibling(pu_own.at[t], pu_in.at[t], u_s.at[t], u_r.at[t])

    def down_y(zs):
        return to_hits(dy_out.at[zs], dy_in.at[zs], dy_s.at[zs], dy_r.at[zs], partner)

    def down_z(zs):
        return to_hits(down_own.at[zs], dz_in.at[z], dz_s.at[zs], dz_r.at[z], zs * 2 + y)

    x_y(z).start()

    @pl.when(z < last)
    def _():
        x_right(z).start()

    @pl.when(z > 0)
    def _():
        x_left(z).start()

    weights[1].wait()
    weights[2].wait()

    @pl.loop(0, outer + 2)
    def _(t):
        @pl.when(z - t - 1 >= 0)
        def _():
            zs = z - t - 1
            x_right(zs).wait_recv()

            @pl.when(z < last)
            def _():
                x_right(zs).start()

        @pl.when(z + t + 1 <= last)
        def _():
            zs = z + t + 1
            x_left(zs).wait_recv()

            @pl.when(z > 0)
            def _():
                x_left(zs).start()

        @pl.when(t < last)
        def _():
            x_y(source(t + 1)).start()

        @pl.when(t < outer)
        def _():
            zs = source(t)
            x_y(zs).wait_recv()
            x = x_in[zs].reshape(2 * blk, width)
            pu_own[t] = jnp.dot(x, wu[...], preferred_element_type=F32)
            units(t).start()

        @pl.when((t >= 1) & (t <= outer))
        def _():
            zs = source(t - 1)
            units(t - 1).wait_recv()
            hidden = jax.nn.gelu(pu_own[t - 1] + pu_in[t - 1]).astype(BF16)
            dy_out[zs] = jnp.dot(hidden[blk:], wd[...], preferred_element_type=F32).astype(BF16)

            @pl.when(t > 1)
            def _():
                down_y(zs).start()

            @pl.when(t == outer)
            def _():
                down_y(z).start()

            down_own[zs] = jnp.dot(hidden[:blk], wd[...], preferred_element_type=F32).astype(BF16)

        @pl.when(t > 2)
        def _():
            zs = source(t - 2)
            down_y(zs).wait_recv()
            both = down_own[zs].astype(F32) + dy_in[zs].astype(F32)
            down_own[zs] = both.astype(BF16)
            down_z(zs).start()

    down_y(z).wait_recv()
    stream[...] = stream[...] + down_own[z].astype(F32) + dy_in[z].astype(F32)

    @pl.loop(1, outer)
    def _(t):
        zs = source(t)
        to_hits(down_own.at[zs], dz_in.at[zs], dz_s.at[zs], dz_r.at[zs], zs * 2 + y).wait_recv()
        stream[...] = stream[...] + dz_in[zs].astype(F32)

    out_ref[...] = stream[...].astype(BF16)

    proj.wait_send()
    squares.wait_send()

    @pl.loop(0, outer)
    def _(t):
        for c in att_y(t):
            c.wait_send()

        x_y(t).wait_send()
        units(t).wait_send()
        down_y(t).wait_send()

        @pl.when(t != z)
        def _():
            down_z(t).wait_send()
            for c in att_z_step(0, t):
                c.wait_send()

        @pl.when((t <= z) & (z < last))
        def _():
            x_right(t).wait_send()

        @pl.when((t >= z) & (z > 0))
        def _():
            x_left(t).wait_send()


def shards(n, queries, keys, values, hit_counts, latents, out_proj, norm_gain, up_proj, down_proj):
    rows, width = queries.shape
    blk = rows // n
    outer = n // 2
    hidden = up_proj.shape[1]
    features = out_proj.shape[1]
    live = lax.broadcasted_iota(jnp.int32, (1, keys.shape[0]), 1) < hit_counts[0]
    bias = jnp.where(live, 0.0, -1e30).astype(F32)
    vmem = pl.BlockSpec(memory_space=pltpu.VMEM)
    hbm = pl.BlockSpec(memory_space=pl.ANY)
    heads = width // HD
    dma = lambda m: pltpu.SemaphoreType.DMA((m,))
    return pl.pallas_call(
        functools.partial(kernel, n),
        out_shape=jax.ShapeDtypeStruct(latents.shape, BF16),
        in_specs=[vmem] * 6 + [hbm] * 3,
        out_specs=vmem,
        scratch_shapes=[
            pltpu.VMEM(out_proj.shape, BF16),
            pltpu.VMEM(up_proj.shape, BF16),
            pltpu.VMEM(down_proj.shape, BF16),
            pltpu.VMEM((outer, blk, width), BF16),
            pltpu.VMEM((outer, blk, width), BF16),
            pltpu.VMEM((outer, blk, width), BF16),
            pltpu.VMEM((2, outer, blk, width), BF16),
            pltpu.VMEM((outer, 2 * heads, blk), F32),
            pltpu.VMEM((outer, 2 * heads, blk), F32),
            pltpu.VMEM((outer, 2 * heads, blk), F32),
            pltpu.VMEM((2, outer, 2 * heads, blk), F32),
            pltpu.VMEM((blk, width), BF16),
            pltpu.VMEM((blk, width), F32),
            pltpu.VMEM((blk, width), F32),
            pltpu.VMEM((blk, LANES), F32),
            pltpu.VMEM((blk, LANES), F32),
            pltpu.VMEM((blk, width), F32),
            pltpu.VMEM((outer, 2, blk, width), BF16),
            pltpu.VMEM((outer, 2 * blk, hidden), F32),
            pltpu.VMEM((outer, 2 * blk, hidden), F32),
            pltpu.VMEM((outer, blk, width), BF16),
            pltpu.VMEM((outer, blk, width), BF16),
            pltpu.VMEM((outer, blk, width), BF16),
            pltpu.VMEM((outer, blk, width), BF16),
            dma(3),
            dma(outer), dma(outer), dma(outer), pltpu.SemaphoreType.DMA((2, outer)),
            dma(outer), dma(outer), dma(outer), pltpu.SemaphoreType.DMA((2, outer)),
            dma(2), dma(2),
            pltpu.SemaphoreType.DMA((2, outer)), dma(outer), dma(outer), dma(outer),
            dma(outer), dma(outer), dma(outer), dma(outer), dma(outer), dma(outer),
        ],
        compiler_params=pltpu.CompilerParams(
            collective_id=0, has_side_effects=True, vmem_limit_bytes=56 * 1024 * 1024
        ),
        cost_estimate=pl.CostEstimate(
            flops=4 * rows * keys.shape[0] * width + 2 * blk * width * features + 4 * rows * width * hidden,
            bytes_accessed=16 * 1024 * 1024,
            transcendentals=rows * keys.shape[0] * (width // HD),
        ),
    )(bias, queries, keys, values, latents, norm_gain[None, :], out_proj, up_proj, down_proj)


def solution(mesh):
    return jax.shard_map(
        functools.partial(shards, mesh.shape["hits"]),
        mesh=mesh,
        in_specs=(
            P("groups", "heads"),
            P(("groups", "hits"), "heads"),
            P(("groups", "hits"), "heads"),
            P(("groups", "hits")),
            P(("groups", "hits"), "heads"),
            P("heads", None),
            P("heads"),
            P("heads", "hits"),
            P("hits", "heads"),
        ),
        out_specs=P(("groups", "hits"), "heads"),
        check_vma=False,
    )
```
